32 devices in a mesh: row: 4 (over y, x), col: 8 (over z, core).
Axes of the slice: x: 2, y: 2, z: 4, core: 2. Of those that a mesh axis runs over, the one named last changes fastest.
Arguments:
- features: bfloat16 [16384, 256], P(('col', 'row')), may hold values from -6 to 6
- weight: bfloat16 [256, 256], replicated, may hold values from -0.375 to 0.375
- tile_values: bfloat16 [16384, 128, 128], P(('row', 'col')), may hold values from -0.046875 to 0.046875
- tile_row: int32 [16384], P(('row', 'col')), may hold values from 0 to 31, as said below
- tile_col: int32 [16384], P(('row', 'col')), may hold values from 0 to 15, as said below
- tile_count: int32 [4, 8], P('row', 'col'), may hold values from 128 to 512, as said below
- cotangent: bfloat16 [16384, 256], P(('row', 'col')), may hold values from -6 to 6
Outputs:
- activated: bfloat16 [16384, 256], P(('row', 'col'))
- grad_features: bfloat16 [16384, 256], P(('col', 'row'))
- grad_weight: float32 [256, 256], replicated
The draws below stay inside these ranges and needn't reach their ends.
Inputs may be any that keep to these rules, and one draw needn't show every extreme that they name: `tile_count`: 512 on at least one device in every draw. Within each device's slots the pairs (tile_row, tile_col) are distinct. Within each device's slots the pairs (tile_row, tile_col) are distinct.
All inputs are finite; a program needn't handle non-finite values.
Results may differ from the reference program's by a relative error of at most 0.024.
Values may be sent and summed in bfloat16 or wider, within the bound.
No kernel may reach another device: no remote copies, remote signals or barrier semaphores. Data moves between devices by JAX's collectives and lax.ppermute only.
A program may use at most 128 MiB of HBM per device.

```python
import jax
import jax.numpy as jnp
from jax import lax

F = 256
TILE = 128
ND = 512
TMAX = 512
NODES = 16384
SLOTS = 16384
N_ROW = 4
N_COL = 8


def tile_places(key):
    row_tiles = ND * N_COL // TILE
    col_tiles = ND * N_ROW // TILE
    device_keys = jax.random.split(jax.random.fold_in(key, 11), N_ROW * N_COL)
    chosen = jax.vmap(lambda subkey: jax.random.permutation(subkey, row_tiles * col_tiles)[:TMAX])(device_keys)
    return (chosen.reshape(-1).astype(jnp.int32), col_tiles)


def draw_tile_row(key, part):
    chosen, col_tiles = tile_places(key)
    return (chosen // col_tiles).astype(jnp.int32)


def draw_tile_col(key, part):
    chosen, col_tiles = tile_places(key)
    return (chosen % col_tiles).astype(jnp.int32)


def draw_tile_count(key, part):
    first_key, second_key = jax.random.split(jax.random.fold_in(key, 5))
    counts = jax.random.randint(first_key, (N_ROW * N_COL,), TMAX // 4, TMAX + 1)
    busiest = jax.random.randint(second_key, (), 0, N_ROW * N_COL)
    counts = jnp.where(jnp.arange(N_ROW * N_COL) == busiest, TMAX, counts)
    return counts.reshape(N_ROW, N_COL).astype(jnp.int32)


def block_levels(key, shape, cuts, smallest, top_value):
    def one(axis_at, blocks):
        draws = jax.random.uniform(jax.random.fold_in(jax.random.fold_in(key, 6), axis_at), (blocks,), jnp.float32, smallest / len(cuts), top_value / len(cuts))
        return jnp.repeat(jnp.exp(draws), shape[axis_at] // blocks).reshape((-1,) + (1,) * (len(shape) - axis_at - 1))

    level = one(*cuts[0])
    for cut in cuts[1:]:
        level = level * one(*cut)
    return level


def gaussian(rng, shape, spread, reach, cuts=(), held_as=jnp.bfloat16):
    drawn = jax.random.normal(rng, shape, jnp.float32) * spread
    if len(cuts) > 0:
        drawn = block_levels(rng, shape, cuts, -0.22, 0.18) * drawn
    return jnp.clip(drawn, min=-reach, max=reach).astype(held_as)


def setup_inputs(seed: int = 0) -> dict:
    keys = jax.random.split(jax.random.key(seed), 8)
    return {
        "features": gaussian(keys[0], (NODES, F), 1.0, 6.0, ((0, 32),)),
        "weight": gaussian(keys[1], (F, F), F ** -0.5, 0.375),
        "tile_values": gaussian(keys[2], (SLOTS, TILE, TILE), (TMAX * TILE * TILE // ND) ** -0.5, 0.046875, ((0, 32),)),
        "tile_row": draw_tile_row(jax.random.fold_in(keys[7], 71), 0),
        "tile_col": draw_tile_col(jax.random.fold_in(keys[7], 71), 0),
        "tile_count": draw_tile_count(jax.random.fold_in(keys[7], 71), 0),
        "cotangent": gaussian(keys[6], (NODES, F), 1.0, 6.0, ((0, 32),)),
    }


def silu_slope(values):
    sigma = jax.nn.sigmoid(values)
    return sigma * (1.0 + values * (1.0 - sigma))


def round_keep(values):
    return lax.optimization_barrier(values.astype(jnp.bfloat16)).astype(jnp.float32)


def reference(features, weight, tile_values, tile_row, tile_col, tile_count, cotangent):
    row_tiles = ND * N_COL // TILE
    col_tiles = ND * N_ROW // TILE
    projected = jnp.dot(features, weight, preferred_element_type=jnp.float32).astype(jnp.bfloat16)
    panel_grid = projected.reshape(N_COL, col_tiles, TILE, F)
    tile_grid = tile_values.reshape(N_ROW, N_COL, TMAX, TILE, TILE)
    row_grid = tile_row.reshape(N_ROW, N_COL, TMAX)
    col_grid = tile_col.reshape(N_ROW, N_COL, TMAX)
    live_grid = (jnp.arange(TMAX, dtype=jnp.int32)[None, None, :] < tile_count[:, :, None]).astype(jnp.float32)

    def forward_term(row_id, col_id):
        blocks = tile_grid[row_id, col_id].astype(jnp.float32)
        fetched = panel_grid[col_id][col_grid[row_id, col_id]].astype(jnp.float32)
        product = jnp.einsum("sab,sbf->saf", blocks, fetched) * live_grid[row_id, col_id][:, None, None]
        part = jnp.zeros((row_tiles, TILE, F), jnp.float32).at[row_grid[row_id, col_id]].add(product)
        return round_keep(part.reshape(row_tiles * TILE, F))

    def row_total(row_id):
        def step(running, col_id):
            return running + forward_term(row_id, col_id), None
        start_value = jnp.zeros((row_tiles * TILE, F), jnp.float32)
        return lax.scan(step, start_value, jnp.arange(N_COL, dtype=jnp.int32))[0]

    summed = lax.map(row_total, jnp.arange(N_ROW, dtype=jnp.int32)).reshape(NODES, F)
    activated = jax.nn.silu(summed).astype(jnp.bfloat16)
    slope = (cotangent.astype(jnp.float32) * silu_slope(summed)).astype(jnp.bfloat16)
    slope_grid = slope.reshape(N_ROW, row_tiles, TILE, F)

    def backward_term(row_id, col_id):
        blocks = tile_grid[row_id, col_id].astype(jnp.float32)
        fetched = slope_grid[row_id][row_grid[row_id, col_id]].astype(jnp.float32)
        product = jnp.einsum("sab,saf->sbf", blocks, fetched) * live_grid[row_id, col_id][:, None, None]
        part = jnp.zeros((col_tiles, TILE, F), jnp.float32).at[col_grid[row_id, col_id]].add(product)
        return round_keep(part.reshape(col_tiles * TILE, F))

    def col_total(col_id):
        def step(running, row_id):
            return running + backward_term(row_id, col_id), None
        start_value = jnp.zeros((col_tiles * TILE, F), jnp.float32)
        return lax.scan(step, start_value, jnp.arange(N_ROW, dtype=jnp.int32))[0]

    grad_nodes = lax.map(col_total, jnp.arange(N_COL, dtype=jnp.int32)).reshape(NODES, F).astype(jnp.bfloat16)
    grad_features = jnp.dot(grad_nodes, weight.T, preferred_element_type=jnp.float32).astype(jnp.bfloat16)
    grad_weight = jnp.dot(features.T, grad_nodes, preferred_element_type=jnp.float32)
    return (activated, grad_features, grad_weight)
```

```python
import functools
import math

import jax
import jax.numpy as jnp
from jax import lax
from jax.experimental import pallas as pl
from jax.experimental.pallas import tpu as pltpu
from jax.sharding import PartitionSpec as P

F32 = jnp.float32
BF16 = jnp.bfloat16
IN_VMEM = pl.BlockSpec(memory_space=pltpu.VMEM)
IN_SMEM = pl.BlockSpec(memory_space=pltpu.SMEM)
IN_PLACE = pl.BlockSpec(memory_space=pl.ANY)
VMEM_LIMIT = 12 * 2**20


def silu_slope(values):
    sigma = jax.nn.sigmoid(values)
    return sigma * (1.0 + values * (1.0 - sigma))


def tile_products(tile_values, fetch_index, place_index, live_mask, source, out_tiles, forward):
    slots = tile_values.shape[0]
    tile_size = tile_values.shape[1]
    hidden = source.shape[-1]
    source_tiles = source.shape[0]
    source_flat = source.reshape(source_tiles, tile_size * hidden)
    group_size = math.gcd(slots, 64)
    turn_count = slots // group_size
    source_ids = jnp.arange(source_tiles, dtype=jnp.int32)
    out_ids = jnp.arange(out_tiles, dtype=jnp.int32)

    def step(running, step_index):
        offset = step_index * group_size
        blocks = lax.dynamic_slice_in_dim(tile_values, offset, group_size, 0)
        take = lax.dynamic_slice_in_dim(fetch_index, offset, group_size, 0)
        place = lax.dynamic_slice_in_dim(place_index, offset, group_size, 0)
        live_part = lax.dynamic_slice_in_dim(live_mask, offset, group_size, 0)
        take_onehot = (take[:, None] == source_ids[None, :]).astype(jnp.bfloat16)
        fetched = jnp.dot(take_onehot, source_flat, preferred_element_type=jnp.float32)
        fetched = fetched.astype(jnp.bfloat16).reshape(group_size, tile_size, hidden)
        if forward:
            product = jnp.einsum(
                "sab,sbf->saf", blocks, fetched, preferred_element_type=jnp.float32
            )
        else:
            product = jnp.einsum(
                "sab,saf->sbf", blocks, fetched, preferred_element_type=jnp.float32
            )
        place_onehot = (place[:, None] == out_ids[None, :]).astype(jnp.float32) * live_part[:, None]
        added = lax.dot_general(
            place_onehot,
            product.reshape(group_size, tile_size * hidden),
            (((0,), (0,)), ((), ())),
            precision=lax.Precision.HIGHEST,
            preferred_element_type=jnp.float32,
        )
        return (running + added, None)

    start_value = jnp.zeros((out_tiles, tile_size * hidden), jnp.float32)
    result = lax.scan(step, start_value, jnp.arange(turn_count, dtype=jnp.int32))[0]
    return result.reshape(out_tiles * tile_size, hidden)


def sparse_body(features, weight, tile_values, tile_row, tile_col, tile_count, cotangent):
    row_count = lax.axis_size("row")
    col_count = lax.axis_size("col")
    node_dev = features.shape[0]
    hidden = features.shape[1]
    tile_size = tile_values.shape[1]
    slots = tile_values.shape[0]
    row_tiles = node_dev * col_count // tile_size
    col_tiles = node_dev * row_count // tile_size
    live_mask = (jnp.arange(slots, dtype=jnp.int32) < tile_count[0, 0]).astype(jnp.float32)
    projected = jnp.dot(features, weight, preferred_element_type=jnp.float32).astype(jnp.bfloat16)
    panel_rows = lax.all_gather(projected, "row", axis=0, tiled=True).reshape(
        col_tiles, tile_size, hidden
    )
    forward_part = tile_products(
        tile_values, tile_col, tile_row, live_mask, panel_rows, row_tiles, True
    )
    forward_part = forward_part.astype(jnp.bfloat16)
    summed = lax.psum_scatter(forward_part, "col", scatter_dimension=0, tiled=True).astype(
        jnp.float32
    )
    activated = jax.nn.silu(summed).astype(jnp.bfloat16)
    slope = (cotangent.astype(jnp.float32) * silu_slope(summed)).astype(jnp.bfloat16)
    slope_full = lax.all_gather(slope, "col", axis=0, tiled=True)
    slope_tiles = slope_full.reshape(row_tiles, tile_size, hidden)
    column_part = tile_products(
        tile_values, tile_row, tile_col, live_mask, slope_tiles, col_tiles, False
    )
    column_part = column_part.astype(jnp.bfloat16)
    grad_nodes = (
        lax.psum_scatter(column_part, "row", scatter_dimension=0, tiled=True)
        .astype(jnp.float32)
        .astype(jnp.bfloat16)
    )
    grad_features = lax.dot_general(
        grad_nodes, weight, (((1,), (1,)), ((), ())), preferred_element_type=jnp.float32
    ).astype(jnp.bfloat16)
    weight_term = lax.dot_general(
        features, grad_nodes, (((0,), (0,)), ((), ())), preferred_element_type=jnp.float32
    )
    grad_weight = lax.psum(weight_term, ("row", "col"))
    return (activated, grad_features, grad_weight)


def kernel_call(kernel, out_shape, arguments, name, flops=0, scratch=(), in_specs=None, after=()):
    count = len(arguments)

    def ordered(*refs):
        kernel(*refs[:count], *refs[count + len(after) :])

    return pl.pallas_call(
        ordered if after else kernel,
        out_shape=out_shape,
        in_specs=(in_specs or [IN_VMEM] * count) + [IN_PLACE] * len(after),
        out_specs=jax.tree.map(lambda _: IN_VMEM, out_shape),
        scratch_shapes=list(scratch),
        compiler_params=pltpu.CompilerParams(vmem_limit_bytes=VMEM_LIMIT),
        cost_estimate=pl.CostEstimate(flops=flops, bytes_accessed=0, transcendentals=0),
        name=name,
    )(*arguments, *after)


def later(values, after):
    return pl.pallas_call(
        lambda *refs: None,
        out_shape=[jax.ShapeDtypeStruct(value.shape, value.dtype) for value in values],
        in_specs=[IN_PLACE] * (len(values) + len(after)),
        out_specs=[IN_PLACE] * len(values),
        input_output_aliases={i: i for i in range(len(values))},
        compiler_params=pltpu.CompilerParams(vmem_limit_bytes=VMEM_LIMIT),
        name="later",
    )(*values, *after)


def held(value):
    return pltpu.with_memory_space_constraint(value, pltpu.VMEM)


def swap(value, axis, distance):
    count = lax.axis_size(axis)
    return lax.ppermute(value, axis, [(i, i ^ distance) for i in range(count)])


def load_kernel(count_ref, row_ref, col_ref, tiles_ref, adjacency_ref, rows_ref, cols_ref, zero_ref, sem, sems):
    slots, tile, _ = tiles_ref.shape
    row_copy = pltpu.make_async_copy(row_ref, rows_ref, sems.at[0])
    col_copy = pltpu.make_async_copy(col_ref, cols_ref, sems.at[1])
    row_copy.start()
    col_copy.start()
    row_flip = lax.axis_index("col") * (adjacency_ref.shape[0] // lax.axis_size("col") // tile)
    col_flip = lax.axis_index("row") * (adjacency_ref.shape[1] // lax.axis_size("row") // tile)
    zero_ref[...] = jnp.zeros_like(zero_ref)
    row_copy.wait()
    col_copy.wait()

    def target(slot):
        top = pl.multiple_of((rows_ref[slot] ^ row_flip) * tile, tile)
        left = pl.multiple_of((cols_ref[slot] ^ col_flip) * tile, tile)
        return adjacency_ref.at[pl.ds(top, tile), pl.ds(left, tile)]

    def live(slot, carry):
        pltpu.make_async_copy(tiles_ref.at[slot], target(slot), sem).start()
        return carry

    def dead(slot, carry):
        pltpu.make_async_copy(zero_ref, target(slot), sem).start()
        return carry

    count = count_ref[0, 0]
    lax.fori_loop(0, count, live, 0)
    lax.fori_loop(count, slots, dead, 0)
    pltpu.make_async_copy(adjacency_ref, adjacency_ref, sem).wait()


def forward_kernel(slots, adjacency_ref, *refs):
    source = jnp.concatenate([ref[...] for ref in refs[:4]], axis=0)
    others, out_refs = refs[4 : -len(slots)], refs[-len(slots) :]
    nodes = refs[0].shape[0]
    for i, slot in enumerate(slots):
        total = jnp.dot(adjacency_ref[nodes * slot : nodes * (slot + 1), :], source, preferred_element_type=F32)
        if others:
            total = total + others[i][...].astype(F32)
        out_refs[i][...] = total.astype(out_refs[i].dtype)


def add_kernel(*refs):
    count = len(refs) // 3
    for mine, other, out in zip(refs[:count], refs[count : 2 * count], refs[2 * count :]):
        out[...] = (mine[...] + other[...].astype(F32)).astype(out.dtype)


def middle_kernel(weight_ref, cotangent_ref, mine_ref, r1_ref, r2_ref, r3_ref,
                  activated_ref, sent_ref, keep_ref, send_ref, term_ref):
    mixed = mine_ref[...] + r1_ref[...].astype(F32) + r2_ref[...].astype(F32) + r3_ref[...].astype(F32)
    mixed = mixed.astype(BF16)
    weight = weight_ref[...]
    summed = jnp.dot(mixed, weight, preferred_element_type=F32)
    sigma = 1.0 / (1.0 + jnp.exp(-summed))
    activated_ref[...] = (summed * sigma).astype(BF16)
    slope = cotangent_ref[...].astype(F32) * sigma * (1.0 + summed * (1.0 - sigma))
    slope = slope.astype(BF16)
    sent_ref[...] = lax.dot_general(
        slope, weight, (((1,), (1,)), ((), ())), preferred_element_type=F32
    ).astype(BF16)
    term_ref[...] = lax.dot_general(mixed, slope, (((0,), (0,)), ((), ())), preferred_element_type=F32)
    half = keep_ref.shape[0]
    core = lax.axis_index("col") % 2
    keep_ref[...] = term_ref[pl.ds(pl.multiple_of(core * half, half), half), :]
    send_ref[...] = term_ref[pl.ds(pl.multiple_of((1 - core) * half, half), half), :]


def backward_block(slots, chunk, nodes, adjacency_ref, source):
    left = nodes * chunk
    block = jnp.concatenate(
        [adjacency_ref[nodes * slot : nodes * (slot + 1), left : left + nodes] for slot in slots], axis=0
    )
    return lax.dot_general(block, source, (((0,), (0,)), ((), ())), preferred_element_type=F32)


def backward_near_kernel(slots, adjacency_ref, *refs):
    source = jnp.concatenate([ref[...] for ref in refs[: len(slots)]], axis=0)
    out_ref = refs[-1]
    nodes = refs[0].shape[0]
    for chunk in range(out_ref.shape[0] // nodes):
        out_ref[nodes * chunk : nodes * (chunk + 1), :] = backward_block(slots, chunk, nodes, adjacency_ref, source)


def backward_home_kernel(slots, adjacency_ref, start_ref, *refs):
    source = jnp.concatenate([ref[...] for ref in refs[: len(slots)]], axis=0)
    out_ref = refs[-1]
    nodes = refs[0].shape[0]
    for chunk in range(out_ref.shape[0] // nodes):
        here = slice(nodes * chunk, nodes * (chunk + 1))
        out_ref[here, :] = start_ref[here, :] + backward_block(slots, chunk, nodes, adjacency_ref, source)


def backward_away_kernel(slots, chunks, adjacency_ref, start_ref, *refs):
    source = jnp.concatenate([ref[...] for ref in refs[: len(slots)]], axis=0)
    nodes = refs[0].shape[0]
    for out_ref, chunk in zip(refs[len(slots) :], chunks):
        here = slice(nodes * chunk, nodes * (chunk + 1))
        total = start_ref[here, :] + backward_block(slots, chunk, nodes, adjacency_ref, source)
        out_ref[...] = total.astype(out_ref.dtype)


def finish_kernel(mine_ref, q1_ref, q2_ref, q3_ref, half_ref, other_ref, nodes_ref, weight_ref):
    total = mine_ref[...] + q1_ref[...].astype(F32) + q2_ref[...].astype(F32) + q3_ref[...].astype(F32)
    nodes_ref[...] = total.astype(nodes_ref.dtype)
    half = half_ref.shape[0]
    core = lax.axis_index("col") % 2
    weight_ref[pl.ds(pl.multiple_of(core * half, half), half), :] = half_ref[...]
    weight_ref[pl.ds(pl.multiple_of((1 - core) * half, half), half), :] = other_ref[...]


def sum_kernel(mine_ref, other_ref, out_ref):
    out_ref[...] = mine_ref[...] + other_ref[...]


def dense_body(features, weight, tile_values, tile_row, tile_col, tile_count, cotangent):
    nodes, hidden = features.shape
    slots, tile = tile_values.shape[:2]
    rows, cols = nodes * lax.axis_size("col"), nodes * lax.axis_size("row")
    block = jax.ShapeDtypeStruct((nodes, hidden), BF16)
    exact = pltpu.VMEM((nodes, hidden), F32)
    running = pltpu.VMEM((cols, hidden), F32)
    whole, half = (jax.ShapeDtypeStruct((hidden // n, hidden), F32) for n in (1, 2))
    slot_flops = 2 * nodes * cols * hidden

    def in_hbm(value):
        return pltpu.with_memory_space_constraint(value, pltpu.HBM)

    adjacency = kernel_call(
        load_kernel,
        pltpu.VMEM((rows, cols), BF16),
        (tile_count, in_hbm(tile_row), in_hbm(tile_col), in_hbm(tile_values)),
        "load_tiles",
        scratch=(
            pltpu.SMEM((slots,), jnp.int32),
            pltpu.SMEM((slots,), jnp.int32),
            pltpu.VMEM((tile, tile), BF16),
            pltpu.SemaphoreType.DMA,
            pltpu.SemaphoreType.DMA((2,)),
        ),
        in_specs=[IN_SMEM, IN_PLACE, IN_PLACE, IN_PLACE],
    )
    adjacency = held(adjacency)
    source = [features] + [swap(features, "row", d) for d in (1, 2, 3)]

    def forward(slot_ids, kind, name, others=(), after=()):
        return kernel_call(
            functools.partial(forward_kernel, slot_ids), [kind] * len(slot_ids) if not isinstance(kind, list) else kind,
            (adjacency, *source, *others), name, flops=slot_flops * len(slot_ids), after=after,
        )

    away_far = [swap(value, "col", 1) for value in forward((7, 5), block, "forward_away_far")]
    home_far = [held(value) for value in forward((6, 4), exact, "forward_home_far")]
    far = kernel_call(add_kernel, [block] * 2, (*home_far, *away_far), "add_far")
    away_near = forward((3, 1), block, "forward_away_near", after=(far[0],))
    away_near = [swap(value, "col", 1) for value in away_near]
    r3, r2 = swap(far[0], "col", 6), swap(far[1], "col", 4)
    near, mine = forward((2, 0), [block, exact], "forward_home_near", others=away_near)
    r1 = swap(near, "col", 2)
    activated, sent, keep, send = kernel_call(
        middle_kernel, [block, block, half, half], (weight, cotangent, held(mine), r1, r2, r3), "middle",
        scratch=(pltpu.VMEM(whole.shape, F32),),
    )

    s3, s2, s1 = (swap(sent, "col", 2 * d) for d in (3, 2, 1))
    o0, o1 = swap(sent, "col", 1), swap(s1, "col", 1)

    def add(value, axis, distance, after=()):
        return kernel_call(sum_kernel, half, (value, swap(value, axis, distance)), "weight_sum", after=after)

    term = kernel_call(sum_kernel, half, (keep, swap(send, "col", 1)), "weight_sum")
    term = add(term, "row", 1)
    term = add(term, "row", 2)
    start = kernel_call(
        functools.partial(backward_near_kernel, (0, 2)), running, (adjacency, sent, s1),
        "backward_home", flops=2 * slot_flops,
    )
    s2, s3 = later((s2, s3), (start, term))
    o2, o3 = swap(s2, "col", 1), swap(s3, "col", 1)
    start = kernel_call(
        functools.partial(backward_home_kernel, (1, 3, 4, 6)), running, (adjacency, held(start), o0, o1, s2, s3),
        "backward_most", flops=4 * slot_flops,
    )
    shares = kernel_call(
        functools.partial(backward_away_kernel, (5, 7), (3, 2, 1)), [block] * 3,
        (adjacency, held(start), o2, o3), "backward_far_away", flops=3 * slot_flops // 2,
    )
    returned = [swap(share, "row", d) for share, d in zip(shares, (3, 2, 1))]
    mine = kernel_call(
        functools.partial(backward_away_kernel, (5, 7), (0,)), [exact],
        (adjacency, held(start), o2, o3), "backward_mine", flops=slot_flops // 2, after=(shares[0],),
    )[0]
    term = add(term, "col", 2, after=(mine,))
    term = add(term, "col", 4)
    grad_features, grad_weight = kernel_call(
        finish_kernel, [block, whole], (held(mine), *returned, term, swap(term, "col", 1)), "finish"
    )
    return (activated, grad_features, grad_weight)


def body(*arguments):
    features, tile_values = arguments[0], arguments[2]
    row_count, col_count = lax.axis_size("row"), lax.axis_size("col")
    cells = (features.shape[0] // tile_values.shape[1]) ** 2 * row_count * col_count
    if cells == tile_values.shape[0] and (row_count, col_count) == (4, 8):
        return dense_body(*arguments)
    return sparse_body(*arguments)


def solution(mesh):
    placed = (
        P(("col", "row"), None),
        P(),
        P(("row", "col"), None, None),
        P(("row", "col")),
        P(("row", "col")),
        P("row", "col"),
        P(("row", "col"), None),
    )
    return jax.shard_map(
        body,
        mesh=mesh,
        in_specs=placed,
        out_specs=(P(("row", "col"), None), P(("col", "row"), None), P()),
        check_vma=False,
    )
```

```python
import functools
import math

import jax
import jax.numpy as jnp
from jax import lax
from jax.experimental import pallas as pl
from jax.experimental.pallas import tpu as pltpu
from jax.sharding import PartitionSpec as P

F32 = jnp.float32
BF16 = jnp.bfloat16
IN_VMEM = pl.BlockSpec(memory_space=pltpu.VMEM)
IN_SMEM = pl.BlockSpec(memory_space=pltpu.SMEM)
IN_PLACE = pl.BlockSpec(memory_space=pl.ANY)
VMEM_LIMIT = 12 * 2**20


def silu_slope(values):
    sigma = jax.nn.sigmoid(values)
    return sigma * (1.0 + values * (1.0 - sigma))


def tile_products(tile_values, fetch_index, place_index, live_mask, source, out_tiles, forward):
    slots = tile_values.shape[0]
    tile_size = tile_values.shape[1]
    hidden = source.shape[-1]
    source_tiles = source.shape[0]
    source_flat = source.reshape(source_tiles, tile_size * hidden)
    group_size = math.gcd(slots, 64)
    turn_count = slots // group_size
    source_ids = jnp.arange(source_tiles, dtype=jnp.int32)
    out_ids = jnp.arange(out_tiles, dtype=jnp.int32)

    def step(running, step_index):
        offset = step_index * group_size
        blocks = lax.dynamic_slice_in_dim(tile_values, offset, group_size, 0)
        take = lax.dynamic_slice_in_dim(fetch_index, offset, group_size, 0)
        place = lax.dynamic_slice_in_dim(place_index, offset, group_size, 0)
        live_part = lax.dynamic_slice_in_dim(live_mask, offset, group_size, 0)
        take_onehot = (take[:, None] == source_ids[None, :]).astype(jnp.bfloat16)
        fetched = jnp.dot(take_onehot, source_flat, preferred_element_type=jnp.float32)
        fetched = fetched.astype(jnp.bfloat16).reshape(group_size, tile_size, hidden)
        if forward:
            product = jnp.einsum(
                "sab,sbf->saf", blocks, fetched, preferred_element_type=jnp.float32
            )
        else:
            product = jnp.einsum(
                "sab,saf->sbf", blocks, fetched, preferred_element_type=jnp.float32
            )
        place_onehot = (place[:, None] == out_ids[None, :]).astype(jnp.float32) * live_part[:, None]
        added = lax.dot_general(
            place_onehot,
            product.reshape(group_size, tile_size * hidden),
            (((0,), (0,)), ((), ())),
            precision=lax.Precision.HIGHEST,
            preferred_element_type=jnp.float32,
        )
        return (running + added, None)

    start_value = jnp.zeros((out_tiles, tile_size * hidden), jnp.float32)
    result = lax.scan(step, start_value, jnp.arange(turn_count, dtype=jnp.int32))[0]
    return result.reshape(out_tiles * tile_size, hidden)


def sparse_body(features, weight, tile_values, tile_row, tile_col, tile_count, cotangent):
    row_count = lax.axis_size("row")
    col_count = lax.axis_size("col")
    node_dev = features.shape[0]
    hidden = features.shape[1]
    tile_size = tile_values.shape[1]
    slots = tile_values.shape[0]
    row_tiles = node_dev * col_count // tile_size
    col_tiles = node_dev * row_count // tile_size
    live_mask = (jnp.arange(slots, dtype=jnp.int32) < tile_count[0, 0]).astype(jnp.float32)
    projected = jnp.dot(features, weight, preferred_element_type=jnp.float32).astype(jnp.bfloat16)
    panel_rows = lax.all_gather(projected, "row", axis=0, tiled=True).reshape(
        col_tiles, tile_size, hidden
    )
    forward_part = tile_products(
        tile_values, tile_col, tile_row, live_mask, panel_rows, row_tiles, True
    )
    forward_part = forward_part.astype(jnp.bfloat16)
    summed = lax.psum_scatter(forward_part, "col", scatter_dimension=0, tiled=True).astype(
        jnp.float32
    )
    activated = jax.nn.silu(summed).astype(jnp.bfloat16)
    slope = (cotangent.astype(jnp.float32) * silu_slope(summed)).astype(jnp.bfloat16)
    slope_full = lax.all_gather(slope, "col", axis=0, tiled=True)
    slope_tiles = slope_full.reshape(row_tiles, tile_size, hidden)
    column_part = tile_products(
        tile_values, tile_row, tile_col, live_mask, slope_tiles, col_tiles, False
    )
    column_part = column_part.astype(jnp.bfloat16)
    grad_nodes = (
        lax.psum_scatter(column_part, "row", scatter_dimension=0, tiled=True)
        .astype(jnp.float32)
        .astype(jnp.bfloat16)
    )
    grad_features = lax.dot_general(
        grad_nodes, weight, (((1,), (1,)), ((), ())), preferred_element_type=jnp.float32
    ).astype(jnp.bfloat16)
    weight_term = lax.dot_general(
        features, grad_nodes, (((0,), (0,)), ((), ())), preferred_element_type=jnp.float32
    )
    grad_weight = lax.psum(weight_term, ("row", "col"))
    return (activated, grad_features, grad_weight)

COVER = 10**10


def kernel_call(kernel, out_shape, arguments, name, flops=0, scratch=(), in_specs=None, after=()):
    count = len(arguments)

    def ordered(*refs):
        kernel(*refs[:count], *refs[count + len(after) :])

    return pl.pallas_call(
        ordered if after else kernel,
        out_shape=out_shape,
        in_specs=(in_specs or [IN_VMEM] * count) + [IN_PLACE] * len(after),
        out_specs=jax.tree.map(lambda _: IN_VMEM, out_shape),
        scratch_shapes=list(scratch),
        compiler_params=pltpu.CompilerParams(vmem_limit_bytes=VMEM_LIMIT),
        cost_estimate=pl.CostEstimate(flops=flops, bytes_accessed=0, transcendentals=0),
        name=name,
    )(*arguments, *after)


def later(values, after, flops=0):
    return pl.pallas_call(
        lambda *refs: None,
        out_shape=[jax.ShapeDtypeStruct(value.shape, value.dtype) for value in values],
        in_specs=[IN_PLACE] * (len(values) + len(after)),
        out_specs=[IN_PLACE] * len(values),
        input_output_aliases={i: i for i in range(len(values))},
        compiler_params=pltpu.CompilerParams(vmem_limit_bytes=VMEM_LIMIT),
        cost_estimate=pl.CostEstimate(flops=flops, bytes_accessed=0, transcendentals=0),
        name="later",
    )(*values, *after)


def held(value):
    return pltpu.with_memory_space_constraint(value, pltpu.VMEM)


def swap(value, axis, distance):
    count = lax.axis_size(axis)
    return lax.ppermute(value, axis, [(i, i ^ distance) for i in range(count)])


def load_kernel(count_ref, row_ref, col_ref, tiles_ref, adjacency_ref, rows_ref, cols_ref, zero_ref, sem, sems):
    slots, tile, _ = tiles_ref.shape
    row_copy = pltpu.make_async_copy(row_ref, rows_ref, sems.at[0])
    col_copy = pltpu.make_async_copy(col_ref, cols_ref, sems.at[1])
    row_copy.start()
    col_copy.start()
    row_flip = lax.axis_index("col") * (adjacency_ref.shape[0] // lax.axis_size("col") // tile)
    col_flip = lax.axis_index("row") * (adjacency_ref.shape[1] // lax.axis_size("row") // tile)
    zero_ref[...] = jnp.zeros_like(zero_ref)
    row_copy.wait()
    col_copy.wait()

    def target(slot):
        top = pl.multiple_of((rows_ref[slot] ^ row_flip) * tile, tile)
        left = pl.multiple_of((cols_ref[slot] ^ col_flip) * tile, tile)
        return adjacency_ref.at[pl.ds(top, tile), pl.ds(left, tile)]

    def live(slot, carry):
        pltpu.make_async_copy(tiles_ref.at[slot], target(slot), sem).start()
        return carry

    def dead(slot, carry):
        pltpu.make_async_copy(zero_ref, target(slot), sem).start()
        return carry

    count = count_ref[0, 0]
    lax.fori_loop(0, count, live, 0)
    lax.fori_loop(count, slots, dead, 0)
    pltpu.make_async_copy(adjacency_ref, adjacency_ref, sem).wait()


def forward_kernel(slots, adjacency_ref, *refs):
    source = jnp.concatenate([ref[...] for ref in refs[:3]], axis=0)
    others, out_refs = refs[4 : -len(slots)], refs[-len(slots) :]
    nodes = refs[0].shape[0]
    for i, slot in enumerate(slots):
        total = jnp.dot(adjacency_ref[nodes * slot : nodes * (slot + 1), nodes:], source, preferred_element_type=F32)
        total = total + refs[3][nodes * slot : nodes * (slot + 1), :]
        if others:
            total = total + others[i][...].astype(F32)
        out_refs[i][...] = total.astype(out_refs[i].dtype)


def forward_own_kernel(adjacency_ref, source_ref, out_ref):
    nodes = source_ref.shape[0]
    for top in range(0, out_ref.shape[0], nodes):
        out_ref[top : top + nodes, :] = jnp.dot(
            adjacency_ref[top : top + nodes, :nodes], source_ref[...], preferred_element_type=F32
        )


def forward_parts_kernel(slots, adjacency_ref, *refs):
    *sources, own_ref = refs[:4]
    source = jnp.concatenate([ref[...] for ref in sources], axis=0)
    nodes = sources[0].shape[0]
    out_refs = refs[4:]
    size = out_refs[0].shape[0]
    for i, out_ref in enumerate(out_refs):
        top = nodes * slots[i * size // nodes] + i * size % nodes
        total = jnp.dot(adjacency_ref[top : top + size, nodes:], source, preferred_element_type=F32)
        out_ref[...] = (total + own_ref[top : top + size, :]).astype(out_ref.dtype)


def forward_home_kernel(adjacency_ref, *refs):
    *sources, own_ref = refs[:4]
    others, near_refs, mine_ref = refs[4:-3], refs[-3:-1], refs[-1]
    source = jnp.concatenate([ref[...] for ref in sources], axis=0)
    nodes = sources[0].shape[0]

    def total(slot, others):
        here = slice(nodes * slot, nodes * (slot + 1))
        value = jnp.dot(adjacency_ref[here, nodes:], source, preferred_element_type=F32) + own_ref[here, :]
        return value + jnp.concatenate([ref[...] for ref in others], axis=0).astype(F32)

    near = total(2, others[: len(others) // 2]).astype(BF16)
    size = near_refs[0].shape[0]
    for i, near_ref in enumerate(near_refs):
        near_ref[...] = near[size * i : size * (i + 1), :]
    mine_ref[...] = total(0, others[len(others) // 2 :])


def add_kernel(*refs):
    count = len(refs) // 3
    for mine, other, out in zip(refs[:count], refs[count : 2 * count], refs[2 * count :]):
        out[...] = (mine[...] + other[...].astype(F32)).astype(out.dtype)


def join_kernel(a_ref, b_ref, out_ref):
    out_ref[...] = a_ref[...].astype(F32) + b_ref[...].astype(F32)


def middle_kernel(weight_ref, cotangent_ref, mine_ref, far_ref, *refs):
    *near_refs, activated_ref, sent_ref, mixed_ref, slope_ref = refs
    near = jnp.concatenate([ref[...] for ref in near_refs], axis=0)
    mixed = mine_ref[...] + near.astype(F32) + far_ref[...]
    mixed = mixed.astype(BF16)
    weight = weight_ref[...]
    summed = jnp.dot(mixed, weight, preferred_element_type=F32)
    sigma = 1.0 / (1.0 + jnp.exp(-summed))
    activated_ref[...] = (summed * sigma).astype(BF16)
    slope = cotangent_ref[...].astype(F32) * sigma * (1.0 + summed * (1.0 - sigma))
    slope = slope.astype(BF16)
    sent_ref[...] = lax.dot_general(
        slope, weight, (((1,), (1,)), ((), ())), preferred_element_type=F32
    ).astype(BF16)
    mixed_ref[...] = mixed
    slope_ref[...] = slope


def term_kernel(mixed_ref, slope_ref, keep_ref, send_ref, term_ref):
    term_ref[...] = lax.dot_general(
        mixed_ref[...], slope_ref[...], (((0,), (0,)), ((), ())), preferred_element_type=F32
    )
    half = keep_ref.shape[0]
    core = lax.axis_index("col") % 2
    keep_ref[...] = term_ref[pl.ds(pl.multiple_of(core * half, half), half), :]
    send_ref[...] = term_ref[pl.ds(pl.multiple_of((1 - core) * half, half), half), :].astype(send_ref.dtype)


def backward_block(slots, chunk, nodes, adjacency_ref, source):
    left = nodes * chunk
    block = jnp.concatenate(
        [adjacency_ref[nodes * slot : nodes * (slot + 1), left : left + nodes] for slot in slots], axis=0
    )
    return lax.dot_general(block, source, (((0,), (0,)), ((), ())), preferred_element_type=F32)


def backward_near_kernel(slots, adjacency_ref, *refs):
    source = jnp.concatenate([ref[...] for ref in refs[: len(slots)]], axis=0)
    out_ref = refs[-1]
    nodes = refs[0].shape[0]
    for chunk in range(out_ref.shape[0] // nodes):
        out_ref[nodes * chunk : nodes * (chunk + 1), :] = backward_block(slots, chunk, nodes, adjacency_ref, source)


def backward_home_kernel(slots, adjacency_ref, start_ref, *refs):
    source = jnp.concatenate([ref[...] for ref in refs[: len(slots)]], axis=0)
    out_ref = refs[-1]
    nodes = refs[0].shape[0]
    for chunk in range(out_ref.shape[0] // nodes):
        here = slice(nodes * chunk, nodes * (chunk + 1))
        out_ref[here, :] = start_ref[here, :] + backward_block(slots, chunk, nodes, adjacency_ref, source)


def backward_away_kernel(slots, chunks, adjacency_ref, start_ref, *refs):
    source = jnp.concatenate([ref[...] for ref in refs[: len(slots)]], axis=0)
    nodes = refs[0].shape[0]
    for out_ref, chunk in zip(refs[len(slots) :], chunks):
        here = slice(nodes * chunk, nodes * (chunk + 1))
        total = start_ref[here, :] + backward_block(slots, chunk, nodes, adjacency_ref, source)
        out_ref[...] = total.astype(out_ref.dtype)


def finish_kernel(mine_ref, q1_ref, q2_ref, q3_ref, half_ref, other_ref, nodes_ref, weight_ref):
    total = mine_ref[...] + q1_ref[...].astype(F32) + q2_ref[...].astype(F32) + q3_ref[...].astype(F32)
    nodes_ref[...] = total.astype(nodes_ref.dtype)
    half = half_ref.shape[0]
    core = lax.axis_index("col") % 2
    weight_ref[pl.ds(pl.multiple_of(core * half, half), half), :] = half_ref[...]
    weight_ref[pl.ds(pl.multiple_of((1 - core) * half, half), half), :] = other_ref[...]


def sum_kernel(mine_ref, other_ref, out_ref):
    out_ref[...] = (mine_ref[...].astype(F32) + other_ref[...].astype(F32)).astype(out_ref.dtype)


def dense_body(features, weight, tile_values, tile_row, tile_col, tile_count, cotangent):
    nodes, hidden = features.shape
    slots, tile = tile_values.shape[:2]
    rows, cols = nodes * lax.axis_size("col"), nodes * lax.axis_size("row")
    block = jax.ShapeDtypeStruct((nodes, hidden), BF16)
    exact = pltpu.VMEM((nodes, hidden), F32)

    def part_of(count):
        return jax.ShapeDtypeStruct((nodes // count, hidden), BF16)

    running = pltpu.VMEM((cols, hidden), F32)
    whole, half = (jax.ShapeDtypeStruct((hidden // n, hidden), F32) for n in (1, 2))

    def in_hbm(value):
        return pltpu.with_memory_space_constraint(value, pltpu.HBM)

    adjacency = kernel_call(
        load_kernel,
        pltpu.VMEM((rows, cols), BF16),
        (tile_count, in_hbm(tile_row), in_hbm(tile_col), in_hbm(tile_values)),
        "load_tiles",
        scratch=(
            pltpu.SMEM((slots,), jnp.int32),
            pltpu.SMEM((slots,), jnp.int32),
            pltpu.VMEM((tile, tile), BF16),
            pltpu.SemaphoreType.DMA,
            pltpu.SemaphoreType.DMA((2,)),
        ),
        in_specs=[IN_SMEM, IN_PLACE, IN_PLACE, IN_PLACE],
    )
    adjacency = held(adjacency)
    source = [swap(features, "row", d) for d in (1, 2, 3)]
    own = kernel_call(
        forward_own_kernel, pltpu.VMEM((rows, hidden), F32), (adjacency, features), "forward_own"
    )
    source.append(held(own))

    def forward(slot_ids, kind, name, others=(), after=()):
        return kernel_call(
            functools.partial(forward_kernel, slot_ids), [kind] * len(slot_ids) if not isinstance(kind, list) else kind,
            (adjacency, *source, *others), name, after=after,
        )

    away_far = [swap(value, "col", 1) for value in forward((7, 5), block, "forward_away_far")]
    home_far = [held(value) for value in forward((6, 4), exact, "forward_home_far")]
    far = kernel_call(add_kernel, [block] * 2, (*home_far, *away_far), "add_far")
    away_near = kernel_call(
        functools.partial(forward_parts_kernel, (3, 1)), [part_of(4)] * (2 * 4), (adjacency, *source), "forward_away_near",
        after=(far[0],),
    )
    away_near = [swap(value, "col", 1) for value in away_near]
    r3, r2 = swap(far[0], "col", 6), swap(far[1], "col", 4)
    *near, mine = kernel_call(
        forward_home_kernel, [part_of(2)] * 2 + [exact], (adjacency, *source, *away_near), "forward_home_near"
    )
    near = [swap(value, "col", 2) for value in near]
    joined = kernel_call(join_kernel, exact, (r2, r3), "join_far", flops=COVER)
    activated, sent, mixed, slope = kernel_call(
        middle_kernel, [block] * 4, (weight, cotangent, held(mine), held(joined), *near), "middle"
    )
    s3, s2, s1 = (swap(sent, "col", 2 * d) for d in (3, 2, 1))
    o0, o1 = swap(sent, "col", 1), swap(s1, "col", 1)

    def add(value, axis, distance, dtype, after=()):
        out_shape = jax.ShapeDtypeStruct(value.shape, dtype)
        return kernel_call(sum_kernel, out_shape, (value, swap(value, axis, distance)), "weight_sum", after=after)

    short = jax.ShapeDtypeStruct(half.shape, BF16)
    keep, send = kernel_call(
        term_kernel, [half, short], (mixed, slope), "weight_term", scratch=(pltpu.VMEM(whole.shape, F32),)
    )
    term = kernel_call(sum_kernel, short, (keep, swap(send, "col", 1)), "weight_sum")
    term = add(term, "row", 1, BF16)
    term = add(term, "row", 2, BF16)
    term = add(term, "col", 2, BF16)
    start = kernel_call(
        functools.partial(backward_near_kernel, (0, 1, 2)), running, (adjacency, sent, o0, s1),
        "backward_home",
    )
    s3, s2 = later((s3, s2), (start,), COVER)
    s3, s2 = later((s3, s2), (term,))
    o2, o3 = swap(s2, "col", 1), swap(s3, "col", 1)
    start = kernel_call(
        functools.partial(backward_home_kernel, (3, 4, 6)), running, (adjacency, held(start), o1, s2, s3),
        "backward_most",
    )
    shares = []
    for chunks in ((3,), (2, 1)):
        shares += kernel_call(
            functools.partial(backward_away_kernel, (5, 7), chunks), [block] * len(chunks),
            (adjacency, held(start), o2, o3), "backward_far_away", after=tuple(shares),
        )
    returned = [swap(share, "row", d) for share, d in zip(shares, (3, 2, 1))]
    mine = kernel_call(
        functools.partial(backward_away_kernel, (5, 7), (0,)), [exact],
        (adjacency, held(start), o2, o3), "backward_mine", after=(shares[0],),
    )[0]
    term = add(later((term,), (mine,))[0], "col", 4, F32)
    grad_features, grad_weight = kernel_call(
        finish_kernel, [block, whole], (held(mine), *returned, term, swap(term, "col", 1)), "finish"
    )
    return (activated, grad_features, grad_weight)


def body(*arguments):
    features, tile_values = arguments[0], arguments[2]
    row_count, col_count = lax.axis_size("row"), lax.axis_size("col")
    cells = (features.shape[0] // tile_values.shape[1]) ** 2 * row_count * col_count
    if cells == tile_values.shape[0] and (row_count, col_count) == (4, 8):
        return dense_body(*arguments)
    return sparse_body(*arguments)


def solution(mesh):
    placed = (
        P(("col", "row"), None),
        P(),
        P(("row", "col"), None, None),
        P(("row", "col")),
        P(("row", "col")),
        P("row", "col"),
        P(("row", "col"), None),
    )
    return jax.shard_map(
        body,
        mesh=mesh,
        in_specs=placed,
        out_specs=(P(("row", "col"), None), P(("col", "row"), None), P()),
        check_vma=False,
    )
```

```python
import functools
import math

import jax
import jax.numpy as jnp
from jax import lax
from jax.experimental import pallas as pl
from jax.experimental.pallas import tpu as pltpu
from jax.sharding import PartitionSpec as P

F32 = jnp.float32
BF16 = jnp.bfloat16
IN_VMEM = pl.BlockSpec(memory_space=pltpu.VMEM)
IN_SMEM = pl.BlockSpec(memory_space=pltpu.SMEM)
IN_PLACE = pl.BlockSpec(memory_space=pl.ANY)
VMEM_LIMIT = 12 * 2**20


def silu_slope(values):
    sigma = jax.nn.sigmoid(values)
    return sigma * (1.0 + values * (1.0 - sigma))


def tile_products(tile_values, fetch_index, place_index, live_mask, source, out_tiles, forward):
    slots = tile_values.shape[0]
    tile_size = tile_values.shape[1]
    hidden = source.shape[-1]
    source_tiles = source.shape[0]
    source_flat = source.reshape(source_tiles, tile_size * hidden)
    group_size = math.gcd(slots, 64)
    turn_count = slots // group_size
    source_ids = jnp.arange(source_tiles, dtype=jnp.int32)
    out_ids = jnp.arange(out_tiles, dtype=jnp.int32)

    def step(running, step_index):
        offset = step_index * group_size
        blocks = lax.dynamic_slice_in_dim(tile_values, offset, group_size, 0)
        take = lax.dynamic_slice_in_dim(fetch_index, offset, group_size, 0)
        place = lax.dynamic_slice_in_dim(place_index, offset, group_size, 0)
        live_part = lax.dynamic_slice_in_dim(live_mask, offset, group_size, 0)
        take_onehot = (take[:, None] == source_ids[None, :]).astype(jnp.bfloat16)
        fetched = jnp.dot(take_onehot, source_flat, preferred_element_type=jnp.float32)
        fetched = fetched.astype(jnp.bfloat16).reshape(group_size, tile_size, hidden)
        if forward:
            product = jnp.einsum(
                "sab,sbf->saf", blocks, fetched, preferred_element_type=jnp.float32
            )
        else:
            product = jnp.einsum(
                "sab,saf->sbf", blocks, fetched, preferred_element_type=jnp.float32
            )
        place_onehot = (place[:, None] == out_ids[None, :]).astype(jnp.float32) * live_part[:, None]
        added = lax.dot_general(
            place_onehot,
            product.reshape(group_size, tile_size * hidden),
            (((0,), (0,)), ((), ())),
            precision=lax.Precision.HIGHEST,
            preferred_element_type=jnp.float32,
        )
        return (running + added, None)

    start_value = jnp.zeros((out_tiles, tile_size * hidden), jnp.float32)
    result = lax.scan(step, start_value, jnp.arange(turn_count, dtype=jnp.int32))[0]
    return result.reshape(out_tiles * tile_size, hidden)


def sparse_body(features, weight, tile_values, tile_row, tile_col, tile_count, cotangent):
    row_count = lax.axis_size("row")
    col_count = lax.axis_size("col")
    node_dev = features.shape[0]
    hidden = features.shape[1]
    tile_size = tile_values.shape[1]
    slots = tile_values.shape[0]
    row_tiles = node_dev * col_count // tile_size
    col_tiles = node_dev * row_count // tile_size
    live_mask = (jnp.arange(slots, dtype=jnp.int32) < tile_count[0, 0]).astype(jnp.float32)
    projected = jnp.dot(features, weight, preferred_element_type=jnp.float32).astype(jnp.bfloat16)
    panel_rows = lax.all_gather(projected, "row", axis=0, tiled=True).reshape(
        col_tiles, tile_size, hidden
    )
    forward_part = tile_products(
        tile_values, tile_col, tile_row, live_mask, panel_rows, row_tiles, True
    )
    forward_part = forward_part.astype(jnp.bfloat16)
    summed = lax.psum_scatter(forward_part, "col", scatter_dimension=0, tiled=True).astype(
        jnp.float32
    )
    activated = jax.nn.silu(summed).astype(jnp.bfloat16)
    slope = (cotangent.astype(jnp.float32) * silu_slope(summed)).astype(jnp.bfloat16)
    slope_full = lax.all_gather(slope, "col", axis=0, tiled=True)
    slope_tiles = slope_full.reshape(row_tiles, tile_size, hidden)
    column_part = tile_products(
        tile_values, tile_row, tile_col, live_mask, slope_tiles, col_tiles, False
    )
    column_part = column_part.astype(jnp.bfloat16)
    grad_nodes = (
        lax.psum_scatter(column_part, "row", scatter_dimension=0, tiled=True)
        .astype(jnp.float32)
        .astype(jnp.bfloat16)
    )
    grad_features = lax.dot_general(
        grad_nodes, weight, (((1,), (1,)), ((), ())), preferred_element_type=jnp.float32
    ).astype(jnp.bfloat16)
    weight_term = lax.dot_general(
        features, grad_nodes, (((0,), (0,)), ((), ())), preferred_element_type=jnp.float32
    )
    grad_weight = lax.psum(weight_term, ("row", "col"))
    return (activated, grad_features, grad_weight)

COVER = 10**10


def kernel_call(kernel, out_shape, arguments, name, flops=0, scratch=(), in_specs=None, after=()):
    count = len(arguments)

    def ordered(*refs):
        kernel(*refs[:count], *refs[count + len(after) :])

    return pl.pallas_call(
        ordered if after else kernel,
        out_shape=out_shape,
        in_specs=(in_specs or [IN_VMEM] * count) + [IN_PLACE] * len(after),
        out_specs=jax.tree.map(lambda _: IN_VMEM, out_shape),
        scratch_shapes=list(scratch),
        compiler_params=pltpu.CompilerParams(vmem_limit_bytes=VMEM_LIMIT),
        cost_estimate=pl.CostEstimate(flops=flops, bytes_accessed=0, transcendentals=0),
        name=name,
    )(*arguments, *after)


def later(values, after, flops=0):
    return pl.pallas_call(
        lambda *refs: None,
        out_shape=[jax.ShapeDtypeStruct(value.shape, value.dtype) for value in values],
        in_specs=[IN_PLACE] * (len(values) + len(after)),
        out_specs=[IN_PLACE] * len(values),
        input_output_aliases={i: i for i in range(len(values))},
        compiler_params=pltpu.CompilerParams(vmem_limit_bytes=VMEM_LIMIT),
        cost_estimate=pl.CostEstimate(flops=flops, bytes_accessed=0, transcendentals=0),
        name="later",
    )(*values, *after)


def held(value):
    return pltpu.with_memory_space_constraint(value, pltpu.VMEM)


def swap(value, axis, distance):
    count = lax.axis_size(axis)
    return lax.ppermute(value, axis, [(i, i ^ distance) for i in range(count)])


def load_kernel(count_ref, row_ref, col_ref, tiles_ref, adjacency_ref, rows_ref, cols_ref, zero_ref, sem, sems):
    slots, tile, _ = tiles_ref.shape
    row_copy = pltpu.make_async_copy(row_ref, rows_ref, sems.at[0])
    col_copy = pltpu.make_async_copy(col_ref, cols_ref, sems.at[1])
    row_copy.start()
    col_copy.start()
    row_flip = lax.axis_index("col") * (adjacency_ref.shape[0] // lax.axis_size("col") // tile)
    col_flip = lax.axis_index("row") * (adjacency_ref.shape[1] // lax.axis_size("row") // tile)
    zero_ref[...] = jnp.zeros_like(zero_ref)
    row_copy.wait()
    col_copy.wait()

    def target(slot):
        top = pl.multiple_of((rows_ref[slot] ^ row_flip) * tile, tile)
        left = pl.multiple_of((cols_ref[slot] ^ col_flip) * tile, tile)
        return adjacency_ref.at[pl.ds(top, tile), pl.ds(left, tile)]

    def live(slot, carry):
        pltpu.make_async_copy(tiles_ref.at[slot], target(slot), sem).start()
        return carry

    def dead(slot, carry):
        pltpu.make_async_copy(zero_ref, target(slot), sem).start()
        return carry

    count = count_ref[0, 0]
    lax.fori_loop(0, count, live, 0)
    lax.fori_loop(count, slots, dead, 0)
    pltpu.make_async_copy(adjacency_ref, adjacency_ref, sem).wait()


def forward_kernel(slots, adjacency_ref, *refs):
    source = jnp.concatenate([ref[...] for ref in refs[:3]], axis=0)
    others, out_refs = refs[4 : -len(slots)], refs[-len(slots) :]
    nodes = refs[0].shape[0]
    for i, slot in enumerate(slots):
        total = jnp.dot(adjacency_ref[nodes * slot : nodes * (slot + 1), nodes:], source, preferred_element_type=F32)
        total = total + refs[3][nodes * slot : nodes * (slot + 1), :]
        if others:
            total = total + others[i][...].astype(F32)
        out_refs[i][...] = total.astype(out_refs[i].dtype)


def forward_own_kernel(adjacency_ref, source_ref, out_ref):
    nodes = source_ref.shape[0]
    for top in range(0, out_ref.shape[0], nodes):
        out_ref[top : top + nodes, :] = jnp.dot(
            adjacency_ref[top : top + nodes, :nodes], source_ref[...], preferred_element_type=F32
        )


def forward_parts_kernel(slots, adjacency_ref, *refs):
    *sources, own_ref = refs[:4]
    source = jnp.concatenate([ref[...] for ref in sources], axis=0)
    nodes = sources[0].shape[0]
    out_refs = refs[4:]
    size = out_refs[0].shape[0]
    for i, out_ref in enumerate(out_refs):
        top = nodes * slots[i * size // nodes] + i * size % nodes
        total = jnp.dot(adjacency_ref[top : top + size, nodes:], source, preferred_element_type=F32)
        out_ref[...] = (total + own_ref[top : top + size, :]).astype(out_ref.dtype)


def forward_home_kernel(adjacency_ref, *refs):
    *sources, own_ref = refs[:4]
    others, near_refs, mine_ref = refs[4:-3], refs[-3:-1], refs[-1]
    source = jnp.concatenate([ref[...] for ref in sources], axis=0)
    nodes = sources[0].shape[0]

    def total(slot, others):
        here = slice(nodes * slot, nodes * (slot + 1))
        value = jnp.dot(adjacency_ref[here, nodes:], source, preferred_element_type=F32) + own_ref[here, :]
        return value + jnp.concatenate([ref[...] for ref in others], axis=0).astype(F32)

    near = total(2, others[: len(others) // 2]).astype(BF16)
    size = near_refs[0].shape[0]
    for i, near_ref in enumerate(near_refs):
        near_ref[...] = near[size * i : size * (i + 1), :]
    mine_ref[...] = total(0, others[len(others) // 2 :])


def add_kernel(*refs):
    count = len(refs) // 3
    for mine, other, out in zip(refs[:count], refs[count : 2 * count], refs[2 * count :]):
        out[...] = (mine[...] + other[...].astype(F32)).astype(out.dtype)


def join_kernel(a_ref, b_ref, out_ref):
    out_ref[...] = a_ref[...].astype(F32) + b_ref[...].astype(F32)


def middle_kernel(weight_ref, cotangent_ref, mine_ref, far_ref, *refs):
    *near_refs, sent_ref, mixed_ref, slope_ref = refs
    near = jnp.concatenate([ref[...] for ref in near_refs], axis=0)
    mixed = mine_ref[...] + near.astype(F32) + far_ref[...]
    mixed = mixed.astype(BF16)
    weight = weight_ref[...]
    summed = jnp.dot(mixed, weight, preferred_element_type=F32)
    sigma = 1.0 / (1.0 + jnp.exp(-summed))
    slope = cotangent_ref[...].astype(F32) * sigma * (1.0 + summed * (1.0 - sigma))
    slope = slope.astype(BF16)
    sent_ref[...] = lax.dot_general(
        slope, weight, (((1,), (1,)), ((), ())), preferred_element_type=F32
    ).astype(BF16)
    mixed_ref[...] = mixed
    slope_ref[...] = slope


def term_kernel(mixed_ref, slope_ref, weight_ref, keep_ref, send_ref, activated_ref, term_ref):
    term_ref[...] = lax.dot_general(
        mixed_ref[...], slope_ref[...], (((0,), (0,)), ((), ())), preferred_element_type=F32
    )
    summed = jnp.dot(mixed_ref[...], weight_ref[...], preferred_element_type=F32)
    activated_ref[...] = (summed / (1.0 + jnp.exp(-summed))).astype(BF16)
    half = keep_ref.shape[0]
    core = lax.axis_index("col") % 2
    keep_ref[...] = term_ref[pl.ds(pl.multiple_of(core * half, half), half), :]
    send_ref[...] = term_ref[pl.ds(pl.multiple_of((1 - core) * half, half), half), :].astype(send_ref.dtype)


def backward_block(slots, chunk, nodes, adjacency_ref, source):
    left = nodes * chunk
    block = jnp.concatenate(
        [adjacency_ref[nodes * slot : nodes * (slot + 1), left : left + nodes] for slot in slots], axis=0
    )
    return lax.dot_general(block, source, (((0,), (0,)), ((), ())), preferred_element_type=F32)


def backward_near_kernel(slots, adjacency_ref, *refs):
    source = jnp.concatenate([ref[...] for ref in refs[: len(slots)]], axis=0)
    out_ref = refs[-1]
    nodes = refs[0].shape[0]
    for chunk in range(out_ref.shape[0] // nodes):
        out_ref[nodes * chunk : nodes * (chunk + 1), :] = backward_block(slots, chunk, nodes, adjacency_ref, source)


def backward_home_kernel(slots, adjacency_ref, start_ref, *refs):
    source = jnp.concatenate([ref[...] for ref in refs[: len(slots)]], axis=0)
    out_ref = refs[-1]
    nodes = refs[0].shape[0]
    for chunk in range(out_ref.shape[0] // nodes):
        here = slice(nodes * chunk, nodes * (chunk + 1))
        out_ref[here, :] = start_ref[here, :] + backward_block(slots, chunk, nodes, adjacency_ref, source)


def backward_away_kernel(slots, chunks, adjacency_ref, start_ref, *refs):
    source = jnp.concatenate([ref[...] for ref in refs[: len(slots)]], axis=0)
    nodes = refs[0].shape[0]
    for out_ref, chunk in zip(refs[len(slots) :], chunks):
        here = slice(nodes * chunk, nodes * (chunk + 1))
        total = start_ref[here, :] + backward_block(slots, chunk, nodes, adjacency_ref, source)
        out_ref[...] = total.astype(out_ref.dtype)


def total_kernel(mine_ref, q1_ref, q2_ref, q3_ref, out_ref):
    total = mine_ref[...] + q1_ref[...].astype(F32) + q2_ref[...].astype(F32) + q3_ref[...].astype(F32)
    out_ref[...] = total.astype(out_ref.dtype)


def halves_kernel(half_ref, other_ref, out_ref):
    half = half_ref.shape[0]
    core = lax.axis_index("col") % 2
    out_ref[pl.ds(pl.multiple_of(core * half, half), half), :] = half_ref[...]
    out_ref[pl.ds(pl.multiple_of((1 - core) * half, half), half), :] = other_ref[...]


def sum_kernel(mine_ref, other_ref, out_ref):
    out_ref[...] = (mine_ref[...].astype(F32) + other_ref[...].astype(F32)).astype(out_ref.dtype)


def dense_body(features, weight, tile_values, tile_row, tile_col, tile_count, cotangent):
    nodes, hidden = features.shape
    slots, tile = tile_values.shape[:2]
    rows, cols = nodes * lax.axis_size("col"), nodes * lax.axis_size("row")
    block = jax.ShapeDtypeStruct((nodes, hidden), BF16)
    exact = pltpu.VMEM((nodes, hidden), F32)

    def part_of(count):
        return jax.ShapeDtypeStruct((nodes // count, hidden), BF16)

    running = pltpu.VMEM((cols, hidden), F32)
    whole, half = (jax.ShapeDtypeStruct((hidden // n, hidden), F32) for n in (1, 2))

    def in_hbm(value):
        return pltpu.with_memory_space_constraint(value, pltpu.HBM)

    adjacency = kernel_call(
        load_kernel,
        pltpu.VMEM((rows, cols), BF16),
        (tile_count, in_hbm(tile_row), in_hbm(tile_col), in_hbm(tile_values)),
        "load_tiles",
        scratch=(
            pltpu.SMEM((slots,), jnp.int32),
            pltpu.SMEM((slots,), jnp.int32),
            pltpu.VMEM((tile, tile), BF16),
            pltpu.SemaphoreType.DMA,
            pltpu.SemaphoreType.DMA((2,)),
        ),
        in_specs=[IN_SMEM, IN_PLACE, IN_PLACE, IN_PLACE],
    )
    adjacency = held(adjacency)
    source = [swap(features, "row", d) for d in (1, 2, 3)]
    own = kernel_call(
        forward_own_kernel, pltpu.VMEM((rows, hidden), F32), (adjacency, features), "forward_own"
    )
    source.append(held(own))

    def forward(slot_ids, kind, name, others=(), after=()):
        return kernel_call(
            functools.partial(forward_kernel, slot_ids), [kind] * len(slot_ids) if not isinstance(kind, list) else kind,
            (adjacency, *source, *others), name, after=after,
        )

    away_far = [swap(value, "col", 1) for value in forward((7, 5), block, "forward_away_far")]
    home_far = [held(value) for value in forward((6, 4), exact, "forward_home_far")]
    far = kernel_call(add_kernel, [block] * 2, (*home_far, *away_far), "add_far")
    away_near = kernel_call(
        functools.partial(forward_parts_kernel, (3, 1)), [part_of(4)] * (2 * 4), (adjacency, *source), "forward_away_near",
        after=(far[0],),
    )
    away_near = [swap(value, "col", 1) for value in away_near]
    r3, r2 = swap(far[0], "col", 6), swap(far[1], "col", 4)
    *near, mine = kernel_call(
        forward_home_kernel, [part_of(2)] * 2 + [exact], (adjacency, *source, *away_near), "forward_home_near"
    )
    near = [swap(value, "col", 2) for value in near]
    joined = kernel_call(join_kernel, exact, (r2, r3), "join_far", flops=COVER)
    sent, mixed, slope = kernel_call(
        middle_kernel, [block] * 3, (weight, cotangent, held(mine), held(joined), *near), "middle"
    )
    s3, s2, s1 = (swap(sent, "col", 2 * d) for d in (3, 2, 1))
    o0, o1 = swap(sent, "col", 1), swap(s1, "col", 1)

    def add(value, axis, distance, dtype, after=()):
        out_shape = jax.ShapeDtypeStruct(value.shape, dtype)
        return kernel_call(sum_kernel, out_shape, (value, swap(value, axis, distance)), "weight_sum", after=after)

    short = jax.ShapeDtypeStruct(half.shape, BF16)
    keep, send, activated = kernel_call(
        term_kernel, [half, short, block], (mixed, slope, weight), "weight_term", scratch=(pltpu.VMEM(whole.shape, F32),)
    )
    term = kernel_call(sum_kernel, short, (keep, swap(send, "col", 1)), "weight_sum")
    term = add(term, "row", 1, BF16)
    term = add(term, "row", 2, BF16)
    term = add(term, "col", 2, BF16)
    start = kernel_call(
        functools.partial(backward_near_kernel, (0, 1, 2)), running, (adjacency, sent, o0, s1),
        "backward_home",
    )
    s3, s2 = later((s3, s2), (start,), COVER)
    s3, s2 = later((s3, s2), (term,))
    o2, o3 = swap(s2, "col", 1), swap(s3, "col", 1)
    start = kernel_call(
        functools.partial(backward_home_kernel, (3, 4, 6)), running, (adjacency, held(start), o1, s2, s3),
        "backward_most",
    )
    shares = []
    for chunks in ((3,), (2, 1)):
        shares += kernel_call(
            functools.partial(backward_away_kernel, (5, 7), chunks), [block] * len(chunks),
            (adjacency, held(start), o2, o3), "backward_far_away", after=tuple(shares),
        )
    returned = [swap(share, "row", d) for share, d in zip(shares, (3, 2, 1))]
    mine = kernel_call(
        functools.partial(backward_away_kernel, (5, 7), (0,)), [exact],
        (adjacency, held(start), o2, o3), "backward_mine", after=(shares[0],),
    )[0]
    term = add(later((term,), (mine,))[0], "col", 4, F32)
    grad_weight = kernel_call(halves_kernel, whole, (term, swap(term, "col", 1)), "weight_halves")
    grad_features = kernel_call(total_kernel, block, (held(mine), *returned), "total")
    return (activated, grad_features, grad_weight)


def body(*arguments):
    features, tile_values = arguments[0], arguments[2]
    row_count, col_count = lax.axis_size("row"), lax.axis_size("col")
    cells = (features.shape[0] // tile_values.shape[1]) ** 2 * row_count * col_count
    if cells == tile_values.shape[0] and (row_count, col_count) == (4, 8):
        return dense_body(*arguments)
    return sparse_body(*arguments)


def solution(mesh):
    placed = (
        P(("col", "row"), None),
        P(),
        P(("row", "col"), None, None),
        P(("row", "col")),
        P(("row", "col")),
        P("row", "col"),
        P(("row", "col"), None),
    )
    return jax.shard_map(
        body,
        mesh=mesh,
        in_specs=placed,
        out_specs=(P(("row", "col"), None), P(("col", "row"), None), P()),
        check_vma=False,
    )
```
